32 devices in a mesh: parts: 2 (over y), blk: 4 (over z), grp: 2 (over x), rep: 2 (over core).
Axes of the slice: x: 2, y: 2, z: 4, core: 2. Of those that a mesh axis runs over, the one named last changes fastest.
Arguments:
- item_factors: bfloat16 [2048, 128], P(('parts', 'blk', 'grp')), parts along dimension 0, may hold values from -0.25 to 0.25
- confidence: bfloat16 [256, 4, 256], P(('parts', 'blk'), None, 'grp'), parts along dimension 0, may hold values from 0.5 to 5
- ratings: bfloat16 [256, 4, 256], P(('parts', 'blk'), None, 'grp'), parts along dimension 0, may hold values from -6 to 6
- pattern: int32 [8, 4, 2], P(('parts', 'blk'), None, 'grp'), parts along dimension 0, may hold values 0 or 1
- counts: int32 [256], P(('parts', 'blk')), parts along dimension 0, may hold values from 1 to 512
Outputs:
- user_factors: float32 [256, 128], P(('parts', 'blk', 'grp'), 'rep'), parts along dimension 0
The draws below stay inside these ranges and needn't reach their ends.
There are 2 independent parts, one for each index of `parts`. The reference program is written for one: setup_inputs(seed, part) draws one part's arguments, and reference() takes and returns one part's arrays. A program takes and returns all parts, laid end to end along the dimension named above; each array names one. Nothing has to cross between parts.
All inputs are finite; a program needn't handle non-finite values. No bound on the sum of `pattern` on one device may be relied on, other than what follows from the above.
Results may differ from the reference program's by a relative error of at most 0.0031.
Values may be sent and summed in bfloat16 or wider, within the bound.
No kernel may reach another device: no remote copies, remote signals or barrier semaphores. Data moves between devices by JAX's collectives and lax.ppermute only.
A program may use at most 64 MiB of HBM per device.

```python
import math
import jax
import jax.numpy as jnp
from jax import lax

D = 128
IB = 128
UB = 32
CG_STEPS = 4
CYCLE = 4
GITEMS = 256
USERS = 128
ITEMS = 1024
N_GRP = 2


def draw_item_factors(key, part):
    key = jax.random.fold_in(key, 7)
    first, second, third = jax.random.split(key, 3)
    columns = jnp.exp(jax.random.uniform(first, (D,), jnp.float32, math.log(0.003), math.log(0.03)))
    base = jnp.clip(jax.random.normal(second, (ITEMS, D), jnp.float32), -4.0, 4.0)
    rows = jnp.exp(jax.random.uniform(third, (ITEMS, 1), jnp.float32, -0.6, 0.6))
    return (base * columns[None, :] * rows).astype(jnp.bfloat16)


def set_ends(values, key, smallest, high):
    dims = values.shape
    place = [jax.random.randint(jax.random.fold_in(key, axis), (), 0, dims[axis]) for axis in range(len(dims))]
    values = values.at[tuple(place)].set(smallest)
    longest = dims.index(max(dims))
    place[longest] = (place[longest] + 1) % dims[longest]
    return values.at[tuple(place)].set(high)


def shard_levels(key, shape, shards, smallest, top_value):
    gain = 1.0
    for position, parts in shards:
        draws = jax.random.uniform(jax.random.fold_in(jax.random.fold_in(key, 6), position), (parts,), jnp.float32, smallest / len(shards), top_value / len(shards))
        gain = gain * jnp.repeat(jnp.exp(draws), shape[position] // parts).reshape((-1,) + (1,) * (len(shape) - 1 - position))
    return gain


def noise(stream_key, extent, width, limit, shards=(), kind=jnp.bfloat16):
    entries = width * jax.random.normal(stream_key, extent, jnp.float32)
    if shards:
        entries = entries * shard_levels(stream_key, extent, shards, -0.22, 0.18)
    return jnp.clip(entries, -limit, limit).astype(kind)


def setup_inputs(seed: int = 0, part: int = 0) -> dict:
    key_of = jax.random.split(jax.random.key(seed), 6)
    part_keys = jax.random.split(jax.random.fold_in(key_of[5], part), 6)
    return {
        "item_factors": draw_item_factors(jax.random.fold_in(jax.random.fold_in(key_of[5], part), 71), part),
        "confidence": jnp.clip(jnp.exp(math.log(5.0) - 2.3025851 * jax.random.uniform(part_keys[1], (USERS, CYCLE, GITEMS), jnp.float32) ** shard_levels(part_keys[1], (USERS, CYCLE, GITEMS), ((0, 4), (2, 2)), -0.2, 0.2)), 0.5, 5.0).astype(jnp.bfloat16),
        "ratings": noise(part_keys[2], (USERS, CYCLE, GITEMS), 1.0, 6.0, ((0, 4), (2, 2))),
        "pattern": set_ends((jax.random.randint(part_keys[3], (CYCLE, CYCLE, N_GRP), 0, 2) < 1).astype(jnp.int32), jax.random.fold_in(part_keys[3], 1), 0, 1),
        "counts": set_ends(jax.random.randint(part_keys[4], (USERS,), 1, 513), jax.random.fold_in(part_keys[4], 1), 1, 512).astype(jnp.int32),
    }


unobserved_weight = 0.25
regular_weight = 0.002
epsilon = 1e-6


def reference(item_factors, confidence, ratings, pattern, counts):
    users = confidence.shape[0]
    cycle_size = pattern.shape[1]
    groups = pattern.shape[2]
    dim = item_factors.shape[1]
    gram = lax.dot_general(item_factors, item_factors, (((0,), (0,)), ((), ())), preferred_element_type=jnp.float32)

    def one_tile(carry, index):
        observed, right_side = carry
        column = (index // groups).astype(jnp.int32)
        group = (index % groups).astype(jnp.int32)
        start = (group * IB).astype(jnp.int32)
        zero = jnp.zeros((), jnp.int32)
        weight_tile = lax.dynamic_slice(confidence, (zero, column, start), (users, 1, IB))[:, 0, :].astype(jnp.float32)
        rating_tile = lax.dynamic_slice(ratings, (zero, column, start), (users, 1, IB))[:, 0, :].astype(jnp.float32)
        flags = lax.dynamic_slice(pattern, (zero, column, group), (cycle_size, 1, 1))[:, 0, 0].astype(jnp.float32)
        mask = jnp.repeat(flags, UB, total_repeat_length=users)
        weighted = weight_tile * mask[:, None]
        row_start = (column * GITEMS + group * IB).astype(jnp.int32)
        factors = lax.dynamic_slice_in_dim(item_factors, row_start, IB, 0)
        scaled = (weighted[:, :, None] * factors.astype(jnp.float32)[None]).astype(jnp.bfloat16)
        observed = observed + jnp.einsum("uik,il->ukl", scaled.astype(jnp.float32), factors.astype(jnp.float32), precision=lax.Precision.HIGHEST)
        paired = (weighted * rating_tile).astype(jnp.bfloat16)
        right_side = right_side + jnp.dot(paired, factors, preferred_element_type=jnp.float32)
        return (observed, right_side), None

    start_state = (jnp.zeros((users, dim, dim), jnp.float32), jnp.zeros((users, dim), jnp.float32))
    (observed, right_side), unused = lax.scan(one_tile, start_state, jnp.arange(cycle_size * groups, dtype=jnp.int32))
    identity = jnp.eye(dim, dtype=jnp.float32)
    normal = unobserved_weight * gram[None] + observed + (regular_weight * counts.astype(jnp.float32))[:, None, None] * identity[None]
    solution = jnp.zeros_like(right_side)
    residual = right_side
    direction = right_side
    norm_now = jnp.sum(residual * residual, axis=1)
    for turn in range(CG_STEPS):
        image = jnp.einsum("ukl,ul->uk", normal, direction, precision=lax.Precision.HIGHEST)
        step_size = norm_now / (jnp.sum(direction * image, axis=1) + epsilon)
        solution = solution + step_size[:, None] * direction
        residual = residual - step_size[:, None] * image
        norm_next = jnp.sum(residual * residual, axis=1)
        direction = residual + (norm_next / (norm_now + epsilon))[:, None] * direction
        norm_now = norm_next
    return solution
```

```python
import functools

import jax
import jax.numpy as jnp
from jax import lax
from jax.experimental import pallas as pl
from jax.experimental.pallas import tpu as pltpu
from jax.sharding import PartitionSpec as P

CG_STEPS = 4

unobserved_weight = 0.25
regular_weight = 0.002
epsilon = 1e-06


def halves(value):
    high = value.astype(jnp.bfloat16)
    low = (value - high.astype(jnp.float32)).astype(jnp.bfloat16)
    return jnp.concatenate([high, low], axis=0)


def joined(value, rows):
    return value[:rows] + value[rows:]


def solve_kernel(half, offset_ref, factors_ref, pair_ref, counts_ref, out_ref):
    factors = factors_ref[...]
    weights = pair_ref[0].astype(jnp.float32) + unobserved_weight
    rows = weights.shape[0]
    ridge = regular_weight * counts_ref[...].astype(jnp.float32)
    right_side = jnp.dot(pair_ref[1], factors, preferred_element_type=jnp.float32)

    def project(direction):
        return joined(
            lax.dot_general(
                halves(direction),
                factors,
                (((1,), (1,)), ((), ())),
                preferred_element_type=jnp.float32,
            ),
            rows,
        )

    def back(values):
        return joined(
            jnp.dot(halves(values), factors, preferred_element_type=jnp.float32),
            rows,
        )

    total = jnp.zeros_like(right_side)
    residual = right_side
    direction = right_side
    norm_now = jnp.sum(residual * residual, axis=1, keepdims=True)
    for turn in range(CG_STEPS):
        image = back(project(direction) * weights) + ridge * direction
        step_size = norm_now / (jnp.sum(direction * image, axis=1, keepdims=True) + epsilon)
        total = total + step_size * direction
        if turn == CG_STEPS - 1:
            break
        residual = residual - step_size * image
        norm_next = jnp.sum(residual * residual, axis=1, keepdims=True)
        direction = residual + (norm_next / (norm_now + epsilon)) * direction
        norm_now = norm_next
    dim = total.shape[1]
    if half == dim:
        out_ref[...] = total
    else:
        core = offset_ref[0]
        chosen = total[:, :half]
        for other in range(1, dim // half):
            chosen = jnp.where(core == other, total[:, other * half : (other + 1) * half], chosen)
        out_ref[...] = chosen


def shards(item_factors, confidence, ratings, pattern, counts):
    tile_items, dim = item_factors.shape
    groups = lax.axis_size("grp")
    group = lax.axis_index("grp")
    cores = lax.axis_size("rep")
    core = lax.axis_index("rep")
    half = dim // cores
    users = confidence.shape[0]
    owned = users // groups
    cycle_size = confidence.shape[1]

    factors = lax.all_gather(item_factors, ("grp", "blk"), axis=0, tiled=True)

    flags = (pattern[0, :, 0] != 0)[None, :, None]
    weight = jnp.where(flags, confidence, jnp.zeros_like(confidence))
    paired = (weight.astype(jnp.float32) * ratings.astype(jnp.float32)).astype(jnp.bfloat16)
    pair = jnp.stack([weight, paired]).reshape(2, groups, owned, cycle_size * tile_items)
    pieces = []
    for distance in range(groups):
        part = lax.dynamic_index_in_dim(pair, (group + distance) % groups, 1, keepdims=False)
        if distance:
            part = lax.ppermute(
                part, "grp", [(i, (i + distance) % groups) for i in range(groups)]
            )
        pieces.append(part)
    received = jnp.stack(pieces)
    order = (group - jnp.arange(groups)) % groups
    received = received[order]
    all_pair = jnp.moveaxis(received, 0, 2).reshape(2, owned, -1)
    owned_counts = lax.dynamic_slice_in_dim(counts, group * owned, owned, 0)[:, None]
    return pl.pallas_call(
        functools.partial(solve_kernel, half),
        out_shape=jax.ShapeDtypeStruct((owned, half), jnp.float32),
        in_specs=[pl.BlockSpec(memory_space=pltpu.SMEM)]
        + [pl.BlockSpec(memory_space=pltpu.VMEM)] * 3,
        out_specs=pl.BlockSpec(memory_space=pltpu.VMEM),
        compiler_params=pltpu.CompilerParams(vmem_limit_bytes=48 * 1024 * 1024),
    )(core[None].astype(jnp.int32), factors, all_pair, owned_counts)


def solution(mesh):
    in_specs = (
        P(("parts", "blk", "grp"), None),
        P(("parts", "blk"), None, "grp"),
        P(("parts", "blk"), None, "grp"),
        P(("parts", "blk"), None, "grp"),
        P(("parts", "blk")),
    )
    out_specs = P(("parts", "blk", "grp"), "rep")
    return jax.shard_map(shards, mesh=mesh, in_specs=in_specs, out_specs=out_specs, check_vma=False)
```

```python
import functools

import jax
import jax.numpy as jnp
from jax import lax
from jax.experimental import pallas as pl
from jax.experimental.pallas import tpu as pltpu
from jax.sharding import PartitionSpec as P

CG_STEPS = 4

unobserved_weight = 0.25
regular_weight = 0.002
epsilon = 1e-06

PLACE = ("blk", "grp", "rep")
LINE = (0, 1, 2, 3)
FOLDED = (0, 1, 3, 2)
EXCHANGES = (
    ((LINE, 2, 0), (LINE, 1, 1)),
    ((LINE, 0, 1), (LINE, 0, 1)),
    ((LINE, 1, 0), (LINE, 3, 1)),
    ((LINE, 3, 0), (LINE, 2, 1)),
)


def stepped(order, position, steps):
    return order[(order.index(position) + steps) % len(order)]


def exchange_route(rules):
    route = []
    for core, (order, steps, other) in enumerate(rules):
        for position in range(4):
            for group in range(2):
                target = stepped(order, position, steps)
                route.append(
                    ((position * 2 + group) * 2 + core, (target * 2 + (group ^ other)) * 2 + core)
                )
    return route


def source_slot(rule, position):
    order, steps, other = rule
    slot = jnp.int32(0)
    for target in range(4):
        slot = jnp.where(position == target, 4 * other + stepped(order, target, -steps), slot)
    return slot


def halves(value):
    high = value.astype(jnp.bfloat16)
    low = (value - high.astype(jnp.float32)).astype(jnp.bfloat16)
    return jnp.concatenate([high, low], axis=0)


def joined(value, rows):
    return value[:rows] + value[rows:]


def conjugate_gradient(factors, weighted, paired, ridge):
    rows = weighted.shape[0]
    weights = weighted + unobserved_weight
    right_side = jnp.dot(paired, factors, preferred_element_type=jnp.float32)

    def project(direction):
        return joined(
            lax.dot_general(
                halves(direction),
                factors,
                (((1,), (1,)), ((), ())),
                preferred_element_type=jnp.float32,
            ),
            rows,
        )

    def back(values):
        return joined(
            jnp.dot(halves(values), factors, preferred_element_type=jnp.float32),
            rows,
        )

    total = jnp.zeros_like(right_side)
    residual = right_side
    direction = right_side
    norm_now = jnp.sum(residual * residual, axis=1, keepdims=True)
    for turn in range(CG_STEPS):
        image = back(project(direction) * weights) + ridge * direction
        step_size = norm_now / (jnp.sum(direction * image, axis=1, keepdims=True) + epsilon)
        total = total + step_size * direction
        if turn == CG_STEPS - 1:
            break
        residual = residual - step_size * image
        norm_next = jnp.sum(residual * residual, axis=1, keepdims=True)
        direction = residual + (norm_next / (norm_now + epsilon)) * direction
        norm_now = norm_next
    return total


def columns_of(total, core, half):
    chosen = total[:, :half]
    for other in range(1, total.shape[1] // half):
        chosen = jnp.where(core == other, total[:, other * half : (other + 1) * half], chosen)
    return chosen


def pair_kernel(flags_ref, confidence_ref, ratings_ref, mine_ref, theirs_ref):
    group = lax.axis_index("grp")
    users, cycle_size, tile_items = confidence_ref.shape
    owned = users // 2
    weight = confidence_ref[...].astype(jnp.float32)
    rating = ratings_ref[...].astype(jnp.float32)
    for source in range(cycle_size):
        flag = flags_ref[source] != 0
        masked = jnp.where(flag, weight[:, source, :], 0.0)
        product = masked * rating[:, source, :]
        for kind, value in enumerate((masked, product)):
            value = value.astype(jnp.bfloat16)
            first, second = value[:owned], value[owned:]
            mine_ref[kind, source] = jnp.where(group == 0, first, second)
            theirs_ref[kind, source] = jnp.where(group == 0, second, first)


def chip_kernel(*refs):
    own_ref, *block_refs, mine_ref, theirs_ref, counts_ref, out_ref, held = refs
    position = lax.axis_index("blk")
    core = lax.axis_index("rep")
    cycle_size, dim = mine_ref.shape[1], own_ref.shape[1]
    held[position] = own_ref[...]
    direct = block_refs[: len(EXCHANGES)]
    passed = list(block_refs[len(EXCHANGES) :])
    for rules, block_ref in zip(EXCHANGES, direct):
        slots = [source_slot(rule, position) for rule in rules]
        held[jnp.where(core == 0, slots[0], slots[1])] = block_ref[...]
        if rules[0] != rules[1]:
            held[jnp.where(core == 0, slots[1], slots[0])] = passed.pop(0)[...]
    factors = held[...].reshape(-1, dim)
    blocks = [ref.at[:, source] for ref in (mine_ref, theirs_ref) for source in range(cycle_size)]
    weighted = jnp.concatenate([block[0] for block in blocks], axis=1).astype(jnp.float32)
    paired = jnp.concatenate([block[1] for block in blocks], axis=1)
    ridge = regular_weight * counts_ref[...].astype(jnp.float32)
    total = conjugate_gradient(factors, weighted, paired, ridge)
    out_ref[...] = columns_of(total, core, out_ref.shape[1])


VMEM = pl.BlockSpec(memory_space=pltpu.VMEM)
SMEM = pl.BlockSpec(memory_space=pltpu.SMEM)


def chip_shards(item_factors, confidence, ratings, pattern, counts):
    tile_items, dim = item_factors.shape
    users, cycle_size = confidence.shape[:2]
    owned = users // 2
    group = lax.axis_index("grp")
    swap = [(0, 1), (1, 0)]
    direct = [lax.ppermute(item_factors, PLACE, exchange_route(rules)) for rules in EXCHANGES]
    passed = [
        lax.ppermute(block, "rep", swap)
        for rules, block in zip(EXCHANGES, direct)
        if rules[0] != rules[1]
    ]
    half_shape = jax.ShapeDtypeStruct((2, cycle_size, owned, tile_items), jnp.bfloat16)
    mine, theirs = pl.pallas_call(
        pair_kernel,
        out_shape=(half_shape, half_shape),
        in_specs=[SMEM, VMEM, VMEM],
        out_specs=(VMEM, VMEM),
        compiler_params=pltpu.CompilerParams(vmem_limit_bytes=8 * 1024 * 1024),
    )(pattern[0, :, 0], confidence, ratings)
    theirs = lax.ppermute(theirs, "grp", swap)
    owned_counts = lax.dynamic_slice_in_dim(counts, group * owned, owned, 0)[:, None]
    return pl.pallas_call(
        chip_kernel,
        out_shape=jax.ShapeDtypeStruct((owned, dim // 2), jnp.float32),
        in_specs=[VMEM] * (4 + len(direct) + len(passed)),
        out_specs=VMEM,
        scratch_shapes=[pltpu.VMEM((2 * cycle_size, tile_items, dim), jnp.bfloat16)],
        compiler_params=pltpu.CompilerParams(vmem_limit_bytes=8 * 1024 * 1024),
    )(item_factors, *direct, *passed, mine, theirs, owned_counts)


def gathered_kernel(factors_ref, pair_ref, counts_ref, out_ref):
    ridge = regular_weight * counts_ref[...].astype(jnp.float32)
    total = conjugate_gradient(
        factors_ref[...], pair_ref[0].astype(jnp.float32), pair_ref[1], ridge
    )
    out_ref[...] = columns_of(total, lax.axis_index("rep"), out_ref.shape[1])


def gathered_shards(item_factors, confidence, ratings, pattern, counts):
    tile_items, dim = item_factors.shape
    groups = lax.axis_size("grp")
    group = lax.axis_index("grp")
    half = dim // lax.axis_size("rep")
    users, cycle_size = confidence.shape[:2]
    owned = users // groups

    factors = lax.all_gather(item_factors, ("grp", "blk"), axis=0, tiled=True)

    flags = (pattern[0, :, 0] != 0)[None, :, None]
    weight = jnp.where(flags, confidence, jnp.zeros_like(confidence))
    paired = (weight.astype(jnp.float32) * ratings.astype(jnp.float32)).astype(jnp.bfloat16)
    pair = jnp.stack([weight, paired]).reshape(2, groups, owned, cycle_size * tile_items)
    pieces = []
    for distance in range(groups):
        part = lax.dynamic_index_in_dim(pair, (group + distance) % groups, 1, keepdims=False)
        if distance:
            part = lax.ppermute(
                part, "grp", [(i, (i + distance) % groups) for i in range(groups)]
            )
        pieces.append(part)
    received = jnp.stack(pieces)[(group - jnp.arange(groups)) % groups]
    all_pair = jnp.moveaxis(received, 0, 2).reshape(2, owned, -1)
    owned_counts = lax.dynamic_slice_in_dim(counts, group * owned, owned, 0)[:, None]
    return pl.pallas_call(
        gathered_kernel,
        out_shape=jax.ShapeDtypeStruct((owned, half), jnp.float32),
        in_specs=[VMEM] * 3,
        out_specs=VMEM,
        compiler_params=pltpu.CompilerParams(vmem_limit_bytes=48 * 1024 * 1024),
    )(factors, all_pair, owned_counts)


def solution(mesh):
    in_specs = (
        P(("parts", "blk", "grp"), None),
        P(("parts", "blk"), None, "grp"),
        P(("parts", "blk"), None, "grp"),
        P(("parts", "blk"), None, "grp"),
        P(("parts", "blk")),
    )
    out_specs = P(("parts", "blk", "grp"), "rep")
    sizes = tuple(mesh.shape[axis] for axis in PLACE)
    shards = chip_shards if sizes == (4, 2, 2) else gathered_shards
    return jax.shard_map(shards, mesh=mesh, in_specs=in_specs, out_specs=out_specs, check_vma=False)
```

```python
import functools

import jax
import jax.numpy as jnp
from jax import lax
from jax.experimental import pallas as pl
from jax.experimental.pallas import tpu as pltpu
from jax.sharding import PartitionSpec as P

CG_STEPS = 4

unobserved_weight = 0.25
regular_weight = 0.002
epsilon = 1e-06

PLACE = ("blk", "grp", "rep")
LINE = (0, 1, 2, 3)
EXCHANGES = (
    ((LINE, 1, 0), (LINE, 2, 0)),
    ((LINE, 1, 1), (LINE, 3, 1)),
    ((LINE, 3, 0), (LINE, 2, 1)),
)


def stepped(order, position, steps):
    return order[(order.index(position) + steps) % len(order)]


def exchange_route(rules):
    route = []
    for core, (order, steps, other) in enumerate(rules):
        for position in range(4):
            for group in range(2):
                target = stepped(order, position, steps)
                route.append(
                    ((position * 2 + group) * 2 + core, (target * 2 + (group ^ other)) * 2 + core)
                )
    return route


def source_slot(rule, position):
    order, steps, other = rule
    slot = jnp.int32(0)
    for target in range(4):
        slot = jnp.where(position == target, 4 * other + stepped(order, target, -steps), slot)
    return slot


def halves(value):
    high = value.astype(jnp.bfloat16)
    low = (value - high.astype(jnp.float32)).astype(jnp.bfloat16)
    return jnp.concatenate([high, low], axis=0)


def joined(value, rows):
    return value[:rows] + value[rows:]


def row_sums(value):
    return jnp.sum(value, axis=1, keepdims=True)


def conjugate_gradient(factors, weighted, paired, ridge):
    rows = weighted.shape[0]
    weights = weighted + unobserved_weight

    def project(vector):
        return joined(
            lax.dot_general(
                halves(vector),
                factors,
                (((1,), (1,)), ((), ())),
                preferred_element_type=jnp.float32,
            ),
            rows,
        )

    def back(values):
        return joined(
            jnp.dot(halves(values), factors, preferred_element_type=jnp.float32),
            rows,
        )

    residual = jnp.dot(paired, factors, preferred_element_type=jnp.float32)
    direction = residual
    projected = project(residual)
    norm_now = row_sums(residual * residual)
    total = jnp.zeros_like(residual)
    for turn in range(CG_STEPS):
        weighed = weights * projected
        curvature = row_sums(weighed * projected) + ridge * row_sums(direction * direction)
        step_size = norm_now / (curvature + epsilon)
        total = total + step_size * direction
        if turn == CG_STEPS - 1:
            break
        residual = residual - step_size * (back(weighed) + ridge * direction)
        norm_next = row_sums(residual * residual)
        ratio = norm_next / (norm_now + epsilon)
        projected = project(residual) + ratio * projected
        direction = residual + ratio * direction
        norm_now = norm_next
    return total


def columns_of(total, core, half):
    chosen = total[:, :half]
    for other in range(1, total.shape[1] // half):
        chosen = jnp.where(core == other, total[:, other * half : (other + 1) * half], chosen)
    return chosen


def packet_kernel(
    flags_ref,
    confidence_ref,
    ratings_ref,
    factors_ref,
    counts_ref,
    earlier_ref,
    mine_ref,
    theirs_ref,
    ridge_ref,
    weight_ref,
    rating_ref,
    count_ref,
    value_ref,
    arrived,
):
    del earlier_ref
    group = lax.axis_index("grp")
    users, cycle_size, tile_items = confidence_ref.shape
    owned = users // 2
    copies = [
        pltpu.make_async_copy(source, target, arrived.at[number])
        for number, (source, target) in enumerate(
            (
                (confidence_ref, weight_ref),
                (ratings_ref, rating_ref),
                (factors_ref, mine_ref.at[pl.ds(0, tile_items)]),
                (factors_ref, theirs_ref.at[pl.ds(0, tile_items)]),
                (counts_ref, count_ref),
            )
        )
    ]
    for copy in copies:
        copy.start()
    copies[0].wait()
    copies[1].wait()
    rows = users * cycle_size
    weight = weight_ref[...].astype(jnp.float32).reshape(rows, tile_items)
    rating = rating_ref[...].astype(jnp.float32).reshape(rows, tile_items)
    source = lax.rem(lax.broadcasted_iota(jnp.int32, (rows, tile_items), 0), cycle_size)
    flag = jnp.zeros_like(source)
    for number in range(cycle_size):
        flag = jnp.where(source == number, flags_ref[number], flag)
    weight = jnp.where(flag != 0, weight, 0.0)
    for kind, value in enumerate((weight, weight * rating)):
        value_ref[kind] = value
        for number in range(cycle_size):
            target = pl.ds(tile_items + (kind * cycle_size + number) * owned, owned)
            for packet_ref, half in ((mine_ref, group), (theirs_ref, 1 - group)):
                start = half * (owned * cycle_size) + number
                packet_ref[target] = value_ref[
                    kind, pl.ds(start, owned, stride=cycle_size)
                ].astype(jnp.bfloat16)
    for copy in copies[2:]:
        copy.wait()
    user = lax.broadcasted_iota(jnp.int32, (owned, users), 0) + group * owned
    entry = lax.broadcasted_iota(jnp.int32, user.shape, 1)
    counts = row_sums(jnp.where(user == entry, count_ref[...].astype(jnp.float32), 0.0))
    ridge_ref[...] = jnp.broadcast_to(regular_weight * counts, ridge_ref.shape)


def chip_kernel(*refs):
    *block_refs, mine_ref, theirs_ref, ridge_ref, out_ref, held = refs
    position = lax.axis_index("blk")
    core = lax.axis_index("rep")
    slots, tile_items, dim = held.shape
    owned, cycle_size = out_ref.shape[0], slots // 2
    for number, rules in enumerate(EXCHANGES):
        places = [source_slot(rule, position) for rule in rules]
        direct, passed = block_refs[number], block_refs[len(EXCHANGES) + number]
        held[jnp.where(core == 0, places[0], places[1])] = direct[...]
        held[jnp.where(core == 0, places[1], places[0])] = passed[...]
    held[position] = mine_ref[:tile_items]
    held[cycle_size + position] = theirs_ref[:tile_items]
    factors = held[...].reshape(-1, dim)

    def joined_tiles(kind):
        rows = [
            pl.ds(tile_items + (kind * cycle_size + source) * owned, owned)
            for source in range(cycle_size)
        ]
        return jnp.concatenate([ref[row] for ref in (mine_ref, theirs_ref) for row in rows], axis=1)

    weighted = joined_tiles(0).astype(jnp.float32)
    total = conjugate_gradient(factors, weighted, joined_tiles(1), ridge_ref[...])
    out_ref[...] = columns_of(total, core, out_ref.shape[1])


VMEM = pl.BlockSpec(memory_space=pltpu.VMEM)
SMEM = pl.BlockSpec(memory_space=pltpu.SMEM)
HBM = pl.BlockSpec(memory_space=pltpu.HBM)


def chip_shards(item_factors, confidence, ratings, pattern, counts):
    tile_items, dim = item_factors.shape
    users, cycle_size = confidence.shape[:2]
    owned = users // 2
    swap = [(0, 1), (1, 0)]
    direct = [lax.ppermute(item_factors, PLACE, exchange_route(rules)) for rules in EXCHANGES]
    passed = [lax.ppermute(block, "rep", swap) for block in direct]
    packet_inputs = (pattern[0, :, 0], confidence, ratings, item_factors, counts[None])
    packet = jax.ShapeDtypeStruct((tile_items + 2 * cycle_size * owned, dim), jnp.bfloat16)
    ridge = jax.ShapeDtypeStruct((owned, dim), jnp.float32)
    mine, theirs, ridge = pl.pallas_call(
        packet_kernel,
        out_shape=(packet, packet, ridge),
        in_specs=[SMEM, HBM, HBM, HBM, HBM, VMEM],
        out_specs=(VMEM, VMEM, VMEM),
        scratch_shapes=[
            pltpu.VMEM(confidence.shape, jnp.bfloat16),
            pltpu.VMEM(ratings.shape, jnp.bfloat16),
            pltpu.VMEM((1, users), jnp.int32),
            pltpu.VMEM((2, users * cycle_size, tile_items), jnp.float32),
            pltpu.SemaphoreType.DMA((5,)),
        ],
        compiler_params=pltpu.CompilerParams(vmem_limit_bytes=8 * 1024 * 1024),
    )(
        *(pltpu.with_memory_space_constraint(array, pltpu.HBM) for array in packet_inputs), direct[0]
    )
    theirs = lax.ppermute(theirs, "grp", swap)
    return pl.pallas_call(
        chip_kernel,
        out_shape=jax.ShapeDtypeStruct((owned, dim // 2), jnp.float32),
        in_specs=[VMEM] * (3 + len(direct) + len(passed)),
        out_specs=VMEM,
        scratch_shapes=[pltpu.VMEM((2 * cycle_size, tile_items, dim), jnp.bfloat16)],
        compiler_params=pltpu.CompilerParams(vmem_limit_bytes=8 * 1024 * 1024),
    )(*direct, *passed, mine, theirs, ridge)


def gathered_kernel(factors_ref, pair_ref, counts_ref, out_ref):
    ridge = regular_weight * counts_ref[...].astype(jnp.float32)
    total = conjugate_gradient(
        factors_ref[...], pair_ref[0].astype(jnp.float32), pair_ref[1], ridge
    )
    out_ref[...] = columns_of(total, lax.axis_index("rep"), out_ref.shape[1])


def gathered_shards(item_factors, confidence, ratings, pattern, counts):
    tile_items, dim = item_factors.shape
    groups = lax.axis_size("grp")
    group = lax.axis_index("grp")
    half = dim // lax.axis_size("rep")
    users, cycle_size = confidence.shape[:2]
    owned = users // groups

    factors = lax.all_gather(item_factors, ("grp", "blk"), axis=0, tiled=True)

    flags = (pattern[0, :, 0] != 0)[None, :, None]
    weight = jnp.where(flags, confidence, jnp.zeros_like(confidence))
    paired = (weight.astype(jnp.float32) * ratings.astype(jnp.float32)).astype(jnp.bfloat16)
    pair = jnp.stack([weight, paired]).reshape(2, groups, owned, cycle_size * tile_items)
    pieces = []
    for distance in range(groups):
        part = lax.dynamic_index_in_dim(pair, (group + distance) % groups, 1, keepdims=False)
        if distance:
            part = lax.ppermute(
                part, "grp", [(i, (i + distance) % groups) for i in range(groups)]
            )
        pieces.append(part)
    received = jnp.stack(pieces)[(group - jnp.arange(groups)) % groups]
    all_pair = jnp.moveaxis(received, 0, 2).reshape(2, owned, -1)
    owned_counts = lax.dynamic_slice_in_dim(counts, group * owned, owned, 0)[:, None]
    return pl.pallas_call(
        gathered_kernel,
        out_shape=jax.ShapeDtypeStruct((owned, half), jnp.float32),
        in_specs=[VMEM] * 3,
        out_specs=VMEM,
        compiler_params=pltpu.CompilerParams(vmem_limit_bytes=48 * 1024 * 1024),
    )(factors, all_pair, owned_counts)


def solution(mesh):
    in_specs = (
        P(("parts", "blk", "grp"), None),
        P(("parts", "blk"), None, "grp"),
        P(("parts", "blk"), None, "grp"),
        P(("parts", "blk"), None, "grp"),
        P(("parts", "blk")),
    )
    out_specs = P(("parts", "blk", "grp"), "rep")
    sizes = tuple(mesh.shape[axis] for axis in PLACE)
    shards = chip_shards if sizes == (4, 2, 2) else gathered_shards
    return jax.shard_map(shards, mesh=mesh, in_specs=in_specs, out_specs=out_specs, check_vma=False)
```

```python
import functools

import jax
import jax.numpy as jnp
from jax import lax
from jax.experimental import pallas as pl
from jax.experimental.pallas import tpu as pltpu
from jax.sharding import PartitionSpec as P

CG_STEPS = 4

unobserved_weight = 0.25
regular_weight = 0.002
epsilon = 1e-06

PLACE = ("blk", "grp", "rep")
ADD, FLIP = "add", "flip"
EXCHANGES = (
    ((FLIP, 1, 1), (ADD, 1, 0)),
    ((FLIP, 2, 1), (FLIP, 3, 1)),
    ((ADD, 3, 0), (ADD, 2, 0)),
)


def stepped(change, position, steps):
    return position ^ abs(steps) if change == FLIP else (position + steps) % 4


def exchange_route(rules):
    route = []
    for core, (change, steps, other) in enumerate(rules):
        for position in range(4):
            for group in range(2):
                target = stepped(change, position, steps)
                route.append(
                    ((position * 2 + group) * 2 + core, (target * 2 + (group ^ other)) * 2 + core)
                )
    return route


def source_slot(rule, position):
    change, steps, other = rule
    if change == FLIP:
        source = lax.bitwise_xor(position, steps)
    else:
        source = lax.bitwise_and(position - steps, 3)
    return 4 * other + source


def halves(value):
    high = value.astype(jnp.bfloat16)
    low = (value - high.astype(jnp.float32)).astype(jnp.bfloat16)
    return jnp.concatenate([high, low], axis=0)


def joined(value, rows):
    return value[:rows] + value[rows:]


def row_sums(value):
    return jnp.sum(value, axis=1, keepdims=True)


def conjugate_gradient(factors, weighted, paired, ridge):
    rows = weighted.shape[0]
    weights = weighted + unobserved_weight

    def project(vector):
        return joined(
            lax.dot_general(
                halves(vector),
                factors,
                (((1,), (1,)), ((), ())),
                preferred_element_type=jnp.float32,
            ),
            rows,
        )

    def back(values):
        return joined(
            jnp.dot(halves(values), factors, preferred_element_type=jnp.float32),
            rows,
        )

    residual = jnp.dot(paired, factors, preferred_element_type=jnp.float32)
    direction = residual
    projected = project(residual)
    norm_now = row_sums(residual * residual)
    total = jnp.zeros_like(residual)
    for turn in range(CG_STEPS):
        weighed = weights * projected
        curvature = row_sums(weighed * projected) + ridge * row_sums(direction * direction)
        step_size = norm_now / (curvature + epsilon)
        total = total + step_size * direction
        if turn == CG_STEPS - 1:
            break
        residual = residual - step_size * (back(weighed) + ridge * direction)
        norm_next = row_sums(residual * residual)
        ratio = norm_next / (norm_now + epsilon)
        projected = project(residual) + ratio * projected
        direction = residual + ratio * direction
        norm_now = norm_next
    return total


def columns_of(total, core, half):
    chosen = total[:, :half]
    for other in range(1, total.shape[1] // half):
        chosen = jnp.where(core == other, total[:, other * half : (other + 1) * half], chosen)
    return chosen


def packet_kernel(
    flags_ref,
    confidence_ref,
    ratings_ref,
    factors_ref,
    counts_ref,
    earlier_ref,
    mine_ref,
    theirs_ref,
    ridge_ref,
    weight_ref,
    rating_ref,
    count_ref,
    value_ref,
    arrived,
):
    del earlier_ref
    group = lax.axis_index("grp")
    users, cycle_size, tile_items = confidence_ref.shape
    owned = users // 2
    copies = [
        pltpu.make_async_copy(source, target, arrived.at[number])
        for number, (source, target) in enumerate(
            (
                (confidence_ref, weight_ref),
                (ratings_ref, rating_ref),
                (factors_ref, mine_ref.at[pl.ds(0, tile_items)]),
                (factors_ref, theirs_ref.at[pl.ds(0, tile_items)]),
                (counts_ref, count_ref),
            )
        )
    ]
    for copy in copies:
        copy.start()
    copies[0].wait()
    copies[1].wait()
    rows = users * cycle_size
    weight = weight_ref[...].astype(jnp.float32).reshape(rows, tile_items)
    rating = rating_ref[...].astype(jnp.float32).reshape(rows, tile_items)
    source = lax.rem(lax.broadcasted_iota(jnp.int32, (rows, tile_items), 0), cycle_size)
    flag = jnp.zeros_like(source)
    for number in range(cycle_size):
        flag = jnp.where(source == number, flags_ref[number], flag)
    weight = jnp.where(flag != 0, weight, 0.0)
    for kind, value in enumerate((weight, weight * rating)):
        value_ref[kind] = value
        for number in range(cycle_size):
            target = pl.ds(tile_items + (kind * cycle_size + number) * owned, owned)
            for packet_ref, half in ((mine_ref, group), (theirs_ref, 1 - group)):
                start = half * (owned * cycle_size) + number
                packet_ref[target] = value_ref[
                    kind, pl.ds(start, owned, stride=cycle_size)
                ].astype(jnp.bfloat16)
    for copy in copies[2:]:
        copy.wait()
    user = lax.broadcasted_iota(jnp.int32, (owned, users), 0) + group * owned
    entry = lax.broadcasted_iota(jnp.int32, user.shape, 1)
    counts = row_sums(jnp.where(user == entry, count_ref[...].astype(jnp.float32), 0.0))
    ridge_ref[...] = jnp.broadcast_to(regular_weight * counts, ridge_ref.shape)


def chip_kernel(*refs):
    *block_refs, mine_ref, theirs_ref, ridge_ref, out_ref, held = refs
    position = lax.axis_index("blk")
    core = lax.axis_index("rep")
    slots, tile_items, dim = held.shape
    owned, cycle_size = out_ref.shape[0], slots // 2
    for number, rules in enumerate(EXCHANGES):
        places = [source_slot(rule, position) for rule in rules]
        direct, passed = block_refs[number], block_refs[len(EXCHANGES) + number]
        held[jnp.where(core == 0, places[0], places[1])] = direct[...]
        held[jnp.where(core == 0, places[1], places[0])] = passed[...]
    held[position] = mine_ref[:tile_items]
    held[cycle_size + position] = theirs_ref[:tile_items]
    factors = held[...].reshape(-1, dim)

    def joined_tiles(kind):
        rows = [
            pl.ds(tile_items + (kind * cycle_size + source) * owned, owned)
            for source in range(cycle_size)
        ]
        return jnp.concatenate([ref[row] for ref in (mine_ref, theirs_ref) for row in rows], axis=1)

    weighted = joined_tiles(0).astype(jnp.float32)
    total = conjugate_gradient(factors, weighted, joined_tiles(1), ridge_ref[...])
    out_ref[...] = columns_of(total, core, out_ref.shape[1])


VMEM = pl.BlockSpec(memory_space=pltpu.VMEM)
SMEM = pl.BlockSpec(memory_space=pltpu.SMEM)
HBM = pl.BlockSpec(memory_space=pltpu.HBM)


def chip_shards(item_factors, confidence, ratings, pattern, counts):
    tile_items, dim = item_factors.shape
    users, cycle_size = confidence.shape[:2]
    owned = users // 2
    swap = [(0, 1), (1, 0)]
    direct = [lax.ppermute(item_factors, PLACE, exchange_route(rules)) for rules in EXCHANGES]
    passed = [lax.ppermute(block, "rep", swap) for block in direct]
    packet_inputs = (pattern[0, :, 0], confidence, ratings, item_factors, counts[None])
    packet = jax.ShapeDtypeStruct((tile_items + 2 * cycle_size * owned, dim), jnp.bfloat16)
    ridge = jax.ShapeDtypeStruct((owned, dim), jnp.float32)
    mine, theirs, ridge = pl.pallas_call(
        packet_kernel,
        out_shape=(packet, packet, ridge),
        in_specs=[SMEM, HBM, HBM, HBM, HBM, VMEM],
        out_specs=(VMEM, VMEM, VMEM),
        scratch_shapes=[
            pltpu.VMEM(confidence.shape, jnp.bfloat16),
            pltpu.VMEM(ratings.shape, jnp.bfloat16),
            pltpu.VMEM((1, users), jnp.int32),
            pltpu.VMEM((2, users * cycle_size, tile_items), jnp.float32),
            pltpu.SemaphoreType.DMA((5,)),
        ],
        compiler_params=pltpu.CompilerParams(vmem_limit_bytes=8 * 1024 * 1024),
    )(
        *(pltpu.with_memory_space_constraint(array, pltpu.HBM) for array in packet_inputs), direct[0]
    )
    theirs = lax.ppermute(theirs, "grp", swap)
    return pl.pallas_call(
        chip_kernel,
        out_shape=jax.ShapeDtypeStruct((owned, dim // 2), jnp.float32),
        in_specs=[VMEM] * (3 + len(direct) + len(passed)),
        out_specs=VMEM,
        scratch_shapes=[pltpu.VMEM((2 * cycle_size, tile_items, dim), jnp.bfloat16)],
        compiler_params=pltpu.CompilerParams(vmem_limit_bytes=8 * 1024 * 1024),
    )(*direct, *passed, mine, theirs, ridge)


def gathered_kernel(factors_ref, pair_ref, counts_ref, out_ref):
    ridge = regular_weight * counts_ref[...].astype(jnp.float32)
    total = conjugate_gradient(
        factors_ref[...], pair_ref[0].astype(jnp.float32), pair_ref[1], ridge
    )
    out_ref[...] = columns_of(total, lax.axis_index("rep"), out_ref.shape[1])


def gathered_shards(item_factors, confidence, ratings, pattern, counts):
    tile_items, dim = item_factors.shape
    groups = lax.axis_size("grp")
    group = lax.axis_index("grp")
    half = dim // lax.axis_size("rep")
    users, cycle_size = confidence.shape[:2]
    owned = users // groups

    factors = lax.all_gather(item_factors, ("grp", "blk"), axis=0, tiled=True)

    flags = (pattern[0, :, 0] != 0)[None, :, None]
    weight = jnp.where(flags, confidence, jnp.zeros_like(confidence))
    paired = (weight.astype(jnp.float32) * ratings.astype(jnp.float32)).astype(jnp.bfloat16)
    pair = jnp.stack([weight, paired]).reshape(2, groups, owned, cycle_size * tile_items)
    pieces = []
    for distance in range(groups):
        part = lax.dynamic_index_in_dim(pair, (group + distance) % groups, 1, keepdims=False)
        if distance:
            part = lax.ppermute(
                part, "grp", [(i, (i + distance) % groups) for i in range(groups)]
            )
        pieces.append(part)
    received = jnp.stack(pieces)[(group - jnp.arange(groups)) % groups]
    all_pair = jnp.moveaxis(received, 0, 2).reshape(2, owned, -1)
    owned_counts = lax.dynamic_slice_in_dim(counts, group * owned, owned, 0)[:, None]
    return pl.pallas_call(
        gathered_kernel,
        out_shape=jax.ShapeDtypeStruct((owned, half), jnp.float32),
        in_specs=[VMEM] * 3,
        out_specs=VMEM,
        compiler_params=pltpu.CompilerParams(vmem_limit_bytes=48 * 1024 * 1024),
    )(factors, all_pair, owned_counts)


def solution(mesh):
    in_specs = (
        P(("parts", "blk", "grp"), None),
        P(("parts", "blk"), None, "grp"),
        P(("parts", "blk"), None, "grp"),
        P(("parts", "blk"), None, "grp"),
        P(("parts", "blk")),
    )
    out_specs = P(("parts", "blk", "grp"), "rep")
    sizes = tuple(mesh.shape[axis] for axis in PLACE)
    shards = chip_shards if sizes == (4, 2, 2) else gathered_shards
    return jax.shard_map(shards, mesh=mesh, in_specs=in_specs, out_specs=out_specs, check_vma=False)
```

```python
import functools

import jax
import jax.numpy as jnp
from jax import lax
from jax.experimental import pallas as pl
from jax.experimental.pallas import tpu as pltpu
from jax.sharding import PartitionSpec as P

CG_STEPS = 4

unobserved_weight = 0.25
regular_weight = 0.002
epsilon = 1e-06

PLACE = ("blk", "grp", "rep")
ADD, FLIP = "add", "flip"
EXCHANGES = (
    ((FLIP, 1, 1), (ADD, 1, 0)),
    ((FLIP, 2, 1), (FLIP, 3, 1)),
    ((ADD, 3, 0), (ADD, 2, 0)),
)


def stepped(change, position, steps):
    return position ^ abs(steps) if change == FLIP else (position + steps) % 4


def exchange_route(rules):
    route = []
    for core, (change, steps, other) in enumerate(rules):
        for position in range(4):
            for group in range(2):
                target = stepped(change, position, steps)
                route.append(
                    ((position * 2 + group) * 2 + core, (target * 2 + (group ^ other)) * 2 + core)
                )
    return route


def source_slot(rule, position):
    change, steps, other = rule
    if change == FLIP:
        source = lax.bitwise_xor(position, steps)
    else:
        source = lax.bitwise_and(position - steps, 3)
    return 4 * other + source


def halves(value):
    high = value.astype(jnp.bfloat16)
    low = (value - high.astype(jnp.float32)).astype(jnp.bfloat16)
    return jnp.concatenate([high, low], axis=0)


def joined(value, rows):
    return value[:rows] + value[rows:]


def row_sums(value):
    return jnp.sum(value, axis=1, keepdims=True)


def conjugate_gradient(factors, weighted, paired, ridge):
    rows = weighted.shape[0]
    weights = weighted + unobserved_weight

    def project(vector):
        return joined(
            lax.dot_general(
                halves(vector),
                factors,
                (((1,), (1,)), ((), ())),
                preferred_element_type=jnp.float32,
            ),
            rows,
        )

    def back(values):
        return joined(
            jnp.dot(halves(values), factors, preferred_element_type=jnp.float32),
            rows,
        )

    residual = jnp.dot(paired, factors, preferred_element_type=jnp.float32)
    direction = residual
    projected = project(residual)
    norm_now = row_sums(residual * residual)
    total = jnp.zeros_like(residual)
    for turn in range(CG_STEPS):
        weighed = weights * projected
        curvature = row_sums(weighed * projected) + ridge * row_sums(direction * direction)
        step_size = norm_now / (curvature + epsilon)
        total = total + step_size * direction
        if turn == CG_STEPS - 1:
            break
        residual = residual - step_size * (back(weighed) + ridge * direction)
        norm_next = row_sums(residual * residual)
        ratio = norm_next / (norm_now + epsilon)
        projected = project(residual) + ratio * projected
        direction = residual + ratio * direction
        norm_now = norm_next
    return total


def columns_of(total, core, half):
    chosen = total[:, :half]
    for other in range(1, total.shape[1] // half):
        chosen = jnp.where(core == other, total[:, other * half : (other + 1) * half], chosen)
    return chosen


def packet_kernel(
    flags_ref,
    confidence_ref,
    ratings_ref,
    factors_ref,
    counts_ref,
    earlier_ref,
    mine_ref,
    theirs_ref,
    ridge_ref,
    weight_ref,
    rating_ref,
    count_ref,
    flag_ref,
    value_ref,
    arrived,
):
    del earlier_ref
    group = lax.axis_index("grp")
    rows, tile_items = confidence_ref.shape
    owned = ridge_ref.shape[0]
    users = 2 * owned
    cycle_size = rows // users
    copies = [
        pltpu.make_async_copy(source, target, arrived.at[number])
        for number, (source, target) in enumerate(
            (
                (confidence_ref, weight_ref),
                (ratings_ref, rating_ref),
                (factors_ref, mine_ref.at[pl.ds(0, tile_items)]),
                (factors_ref, theirs_ref.at[pl.ds(0, tile_items)]),
                (counts_ref, count_ref),
                (flags_ref, flag_ref),
            )
        )
    ]
    for copy in copies:
        copy.start()
    copies[0].wait()
    copies[1].wait()
    copies[5].wait()
    weight = weight_ref[...].astype(jnp.float32)
    rating = rating_ref[...].astype(jnp.float32)
    source = lax.rem(lax.broadcasted_iota(jnp.int32, (rows, tile_items), 0), cycle_size)
    flag = jnp.zeros_like(source)
    for number in range(cycle_size):
        flag = jnp.where(source == number, flag_ref[number], flag)
    weight = jnp.where(flag != 0, weight, 0.0)
    for kind, value in enumerate((weight, weight * rating)):
        value_ref[kind] = value
        for number in range(cycle_size):
            target = pl.ds(tile_items + (kind * cycle_size + number) * owned, owned)
            for packet_ref, half in ((mine_ref, group), (theirs_ref, 1 - group)):
                start = half * (owned * cycle_size) + number
                packet_ref[target] = value_ref[
                    kind, pl.ds(start, owned, stride=cycle_size)
                ].astype(jnp.bfloat16)
    for copy in copies[2:5]:
        copy.wait()
    user = lax.broadcasted_iota(jnp.int32, (owned, users), 0) + group * owned
    entry = lax.broadcasted_iota(jnp.int32, user.shape, 1)
    counts = row_sums(jnp.where(user == entry, count_ref[...].astype(jnp.float32), 0.0))
    ridge_ref[...] = jnp.broadcast_to(regular_weight * counts, ridge_ref.shape)


def chip_kernel(*refs):
    *block_refs, mine_ref, theirs_ref, ridge_ref, out_ref, held = refs
    position = lax.axis_index("blk")
    core = lax.axis_index("rep")
    slots, tile_items, dim = held.shape
    owned, cycle_size = out_ref.shape[0], slots // 2
    for number, rules in enumerate(EXCHANGES):
        places = [source_slot(rule, position) for rule in rules]
        direct, passed = block_refs[number], block_refs[len(EXCHANGES) + number]
        held[jnp.where(core == 0, places[0], places[1])] = direct[...]
        held[jnp.where(core == 0, places[1], places[0])] = passed[...]
    held[position] = mine_ref[:tile_items]
    held[cycle_size + position] = theirs_ref[:tile_items]
    factors = held[...].reshape(-1, dim)

    def joined_tiles(kind):
        rows = [
            pl.ds(tile_items + (kind * cycle_size + source) * owned, owned)
            for source in range(cycle_size)
        ]
        return jnp.concatenate([ref[row] for ref in (mine_ref, theirs_ref) for row in rows], axis=1)

    weighted = joined_tiles(0).astype(jnp.float32)
    total = conjugate_gradient(factors, weighted, joined_tiles(1), ridge_ref[...])
    out_ref[...] = columns_of(total, core, out_ref.shape[1])


VMEM = pl.BlockSpec(memory_space=pltpu.VMEM)
HBM = pl.BlockSpec(memory_space=pltpu.HBM)


def chip_shards(item_factors, confidence, ratings, pattern, counts):
    tile_items, dim = item_factors.shape
    users, cycle_size = confidence.shape[:2]
    owned = users // 2
    swap = [(0, 1), (1, 0)]
    direct = [lax.ppermute(item_factors, PLACE, exchange_route(rules)) for rules in EXCHANGES]
    passed = [lax.ppermute(block, "rep", swap) for block in direct]
    rows = (users * cycle_size, tile_items)
    packet_inputs = (
        pattern[0, :, 0],
        confidence.reshape(rows),
        ratings.reshape(rows),
        item_factors,
        counts[None],
    )
    packet = jax.ShapeDtypeStruct((tile_items + 2 * cycle_size * owned, dim), jnp.bfloat16)
    ridge = jax.ShapeDtypeStruct((owned, dim), jnp.float32)
    mine, theirs, ridge = pl.pallas_call(
        packet_kernel,
        out_shape=(packet, packet, ridge),
        in_specs=[HBM] * 5 + [VMEM],
        out_specs=(VMEM, VMEM, VMEM),
        scratch_shapes=[
            pltpu.VMEM(rows, jnp.bfloat16),
            pltpu.VMEM(rows, jnp.bfloat16),
            pltpu.VMEM((1, users), jnp.int32),
            pltpu.SMEM((cycle_size,), jnp.int32),
            pltpu.VMEM((2, *rows), jnp.float32),
            pltpu.SemaphoreType.DMA((6,)),
        ],
        compiler_params=pltpu.CompilerParams(vmem_limit_bytes=8 * 1024 * 1024),
    )(
        *(pltpu.with_memory_space_constraint(array, pltpu.HBM) for array in packet_inputs), direct[0]
    )
    theirs = lax.ppermute(theirs, "grp", swap)
    return pl.pallas_call(
        chip_kernel,
        out_shape=jax.ShapeDtypeStruct((owned, dim // 2), jnp.float32),
        in_specs=[VMEM] * (3 + len(direct) + len(passed)),
        out_specs=VMEM,
        scratch_shapes=[pltpu.VMEM((2 * cycle_size, tile_items, dim), jnp.bfloat16)],
        compiler_params=pltpu.CompilerParams(vmem_limit_bytes=8 * 1024 * 1024),
    )(*direct, *passed, mine, theirs, ridge)


def gathered_kernel(factors_ref, pair_ref, counts_ref, out_ref):
    ridge = regular_weight * counts_ref[...].astype(jnp.float32)
    total = conjugate_gradient(
        factors_ref[...], pair_ref[0].astype(jnp.float32), pair_ref[1], ridge
    )
    out_ref[...] = columns_of(total, lax.axis_index("rep"), out_ref.shape[1])


def gathered_shards(item_factors, confidence, ratings, pattern, counts):
    tile_items, dim = item_factors.shape
    groups = lax.axis_size("grp")
    group = lax.axis_index("grp")
    half = dim // lax.axis_size("rep")
    users, cycle_size = confidence.shape[:2]
    owned = users // groups

    factors = lax.all_gather(item_factors, ("grp", "blk"), axis=0, tiled=True)

    flags = (pattern[0, :, 0] != 0)[None, :, None]
    weight = jnp.where(flags, confidence, jnp.zeros_like(confidence))
    paired = (weight.astype(jnp.float32) * ratings.astype(jnp.float32)).astype(jnp.bfloat16)
    pair = jnp.stack([weight, paired]).reshape(2, groups, owned, cycle_size * tile_items)
    pieces = []
    for distance in range(groups):
        part = lax.dynamic_index_in_dim(pair, (group + distance) % groups, 1, keepdims=False)
        if distance:
            part = lax.ppermute(
                part, "grp", [(i, (i + distance) % groups) for i in range(groups)]
            )
        pieces.append(part)
    received = jnp.stack(pieces)[(group - jnp.arange(groups)) % groups]
    all_pair = jnp.moveaxis(received, 0, 2).reshape(2, owned, -1)
    owned_counts = lax.dynamic_slice_in_dim(counts, group * owned, owned, 0)[:, None]
    return pl.pallas_call(
        gathered_kernel,
        out_shape=jax.ShapeDtypeStruct((owned, half), jnp.float32),
        in_specs=[VMEM] * 3,
        out_specs=VMEM,
        compiler_params=pltpu.CompilerParams(vmem_limit_bytes=48 * 1024 * 1024),
    )(factors, all_pair, owned_counts)


def solution(mesh):
    in_specs = (
        P(("parts", "blk", "grp"), None),
        P(("parts", "blk"), None, "grp"),
        P(("parts", "blk"), None, "grp"),
        P(("parts", "blk"), None, "grp"),
        P(("parts", "blk")),
    )
    out_specs = P(("parts", "blk", "grp"), "rep")
    sizes = tuple(mesh.shape[axis] for axis in PLACE)
    shards = chip_shards if sizes == (4, 2, 2) else gathered_shards
    return jax.shard_map(shards, mesh=mesh, in_specs=in_specs, out_specs=out_specs, check_vma=False)
```

```python
import functools

import jax
import jax.numpy as jnp
from jax import lax
from jax.experimental import pallas as pl
from jax.experimental.pallas import tpu as pltpu
from jax.sharding import PartitionSpec as P

CG_STEPS = 4

unobserved_weight = 0.25
regular_weight = 0.002
epsilon = 1e-06

PLACE = ("blk", "grp", "rep")
ADD, FLIP = "add", "flip"
EXCHANGES = (
    ((FLIP, 1, 1), (ADD, 1, 0), 1),
    ((FLIP, 2, 1), (FLIP, 3, 1), 0),
    ((ADD, 3, 0), (ADD, 2, 0), 0),
)
PACKET_ACROSS = 1


def stepped(change, position, steps):
    return position ^ abs(steps) if change == FLIP else (position + steps) % 4


def exchange_route(rules):
    route = []
    *rules, across = rules
    for core, (change, steps, other) in enumerate(rules):
        for position in range(4):
            for group in range(2):
                target = stepped(change, position, steps)
                route.append(
                    (
                        (position * 2 + group) * 2 + core,
                        (target * 2 + (group ^ other)) * 2 + (core ^ across),
                    )
                )
    return route


def source_slot(rule, position):
    change, steps, other = rule
    if change == FLIP:
        source = lax.bitwise_xor(position, steps)
    else:
        source = lax.bitwise_and(position - steps, 3)
    return 4 * other + source


def halves(value):
    high = value.astype(jnp.bfloat16)
    low = (value - high.astype(jnp.float32)).astype(jnp.bfloat16)
    return jnp.concatenate([high, low], axis=0)


def joined(value, rows):
    return value[:rows] + value[rows:]


def row_sums(value):
    return jnp.sum(value, axis=1, keepdims=True)


def conjugate_gradient(factors, weighted, paired, ridge):
    rows = weighted.shape[0]
    weights = weighted + unobserved_weight

    def project(vector):
        return joined(
            lax.dot_general(
                halves(vector),
                factors,
                (((1,), (1,)), ((), ())),
                preferred_element_type=jnp.float32,
            ),
            rows,
        )

    def back(values):
        return joined(
            jnp.dot(halves(values), factors, preferred_element_type=jnp.float32),
            rows,
        )

    residual = jnp.dot(paired, factors, preferred_element_type=jnp.float32)
    direction = residual
    projected = project(residual)
    norm_now = row_sums(residual * residual)
    total = jnp.zeros_like(residual)
    for turn in range(CG_STEPS):
        weighed = weights * projected
        curvature = row_sums(weighed * projected) + ridge * row_sums(direction * direction)
        step_size = norm_now / (curvature + epsilon)
        total = total + step_size * direction
        if turn == CG_STEPS - 1:
            break
        residual = residual - step_size * (back(weighed) + ridge * direction)
        norm_next = row_sums(residual * residual)
        ratio = norm_next / (norm_now + epsilon)
        projected = project(residual) + ratio * projected
        direction = residual + ratio * direction
        norm_now = norm_next
    return total


def columns_of(total, core, half):
    chosen = total[:, :half]
    for other in range(1, total.shape[1] // half):
        chosen = jnp.where(core == other, total[:, other * half : (other + 1) * half], chosen)
    return chosen


def packet_kernel(
    flags_ref,
    confidence_ref,
    ratings_ref,
    factors_ref,
    counts_ref,
    earlier_ref,
    mine_ref,
    theirs_ref,
    ridge_ref,
    weight_ref,
    rating_ref,
    count_ref,
    flag_ref,
    value_ref,
    arrived,
):
    del earlier_ref
    group = lax.axis_index("grp")
    rows, tile_items = confidence_ref.shape
    owned = ridge_ref.shape[0]
    users = 2 * owned
    cycle_size = rows // users
    copies = [
        pltpu.make_async_copy(source, target, arrived.at[number])
        for number, (source, target) in enumerate(
            (
                (confidence_ref, weight_ref),
                (ratings_ref, rating_ref),
                (factors_ref, mine_ref.at[pl.ds(0, tile_items)]),
                (factors_ref, theirs_ref.at[pl.ds(0, tile_items)]),
                (counts_ref, count_ref),
                (flags_ref, flag_ref),
            )
        )
    ]
    for copy in copies:
        copy.start()
    copies[0].wait()
    copies[1].wait()
    copies[5].wait()
    weight = weight_ref[...].astype(jnp.float32)
    rating = rating_ref[...].astype(jnp.float32)
    source = lax.rem(lax.broadcasted_iota(jnp.int32, (rows, tile_items), 0), cycle_size)
    flag = jnp.zeros_like(source)
    for number in range(cycle_size):
        flag = jnp.where(source == number, flag_ref[number], flag)
    weight = jnp.where(flag != 0, weight, 0.0)
    for kind, value in enumerate((weight, weight * rating)):
        value_ref[kind] = value
        for number in range(cycle_size):
            target = pl.ds(tile_items + (kind * cycle_size + number) * owned, owned)
            for packet_ref, half in ((mine_ref, group), (theirs_ref, 1 - group)):
                start = half * (owned * cycle_size) + number
                packet_ref[target] = value_ref[
                    kind, pl.ds(start, owned, stride=cycle_size)
                ].astype(jnp.bfloat16)
    for copy in copies[2:5]:
        copy.wait()
    user = lax.broadcasted_iota(jnp.int32, (owned, users), 0) + group * owned
    entry = lax.broadcasted_iota(jnp.int32, user.shape, 1)
    counts = row_sums(jnp.where(user == entry, count_ref[...].astype(jnp.float32), 0.0))
    ridge_ref[...] = jnp.broadcast_to(regular_weight * counts, ridge_ref.shape)


def chip_kernel(*refs):
    *block_refs, mine_ref, theirs_ref, ridge_ref, out_ref, held = refs
    position = lax.axis_index("blk")
    core = lax.axis_index("rep")
    slots, tile_items, dim = held.shape
    owned, cycle_size = out_ref.shape[0], slots // 2
    for number, rules in enumerate(EXCHANGES):
        *rules, across = rules
        places = [source_slot(rule, position) for rule in rules]
        places = places[::-1] if across else places
        direct, passed = block_refs[number], block_refs[len(EXCHANGES) + number]
        held[jnp.where(core == 0, places[0], places[1])] = direct[...]
        held[jnp.where(core == 0, places[1], places[0])] = passed[...]
    held[position] = mine_ref[:tile_items]
    held[cycle_size + position] = theirs_ref[:tile_items]
    factors = held[...].reshape(-1, dim)

    def joined_tiles(kind):
        rows = [
            pl.ds(tile_items + (kind * cycle_size + source) * owned, owned)
            for source in range(cycle_size)
        ]
        return jnp.concatenate([ref[row] for ref in (mine_ref, theirs_ref) for row in rows], axis=1)

    weighted = joined_tiles(0).astype(jnp.float32)
    total = conjugate_gradient(factors, weighted, joined_tiles(1), ridge_ref[...])
    out_ref[...] = columns_of(total, core, out_ref.shape[1])


VMEM = pl.BlockSpec(memory_space=pltpu.VMEM)
HBM = pl.BlockSpec(memory_space=pltpu.HBM)


def chip_shards(item_factors, confidence, ratings, pattern, counts):
    tile_items, dim = item_factors.shape
    users, cycle_size = confidence.shape[:2]
    owned = users // 2
    swap = [(0, 1), (1, 0)]
    direct = [lax.ppermute(item_factors, PLACE, exchange_route(rules)) for rules in EXCHANGES]
    passed = [lax.ppermute(block, "rep", swap) for block in direct]
    rows = (users * cycle_size, tile_items)
    packet_inputs = (
        pattern[0, :, 0],
        confidence.reshape(rows),
        ratings.reshape(rows),
        item_factors,
        counts[None],
    )
    packet = jax.ShapeDtypeStruct((tile_items + 2 * cycle_size * owned, dim), jnp.bfloat16)
    ridge = jax.ShapeDtypeStruct((owned, dim), jnp.float32)
    mine, theirs, ridge = pl.pallas_call(
        packet_kernel,
        out_shape=(packet, packet, ridge),
        in_specs=[HBM] * 5 + [VMEM],
        out_specs=(VMEM, VMEM, VMEM),
        scratch_shapes=[
            pltpu.VMEM(rows, jnp.bfloat16),
            pltpu.VMEM(rows, jnp.bfloat16),
            pltpu.VMEM((1, users), jnp.int32),
            pltpu.SMEM((cycle_size,), jnp.int32),
            pltpu.VMEM((2, *rows), jnp.float32),
            pltpu.SemaphoreType.DMA((6,)),
        ],
        compiler_params=pltpu.CompilerParams(vmem_limit_bytes=8 * 1024 * 1024),
    )(
        *(pltpu.with_memory_space_constraint(array, pltpu.HBM) for array in packet_inputs), direct[0]
    )
    theirs = lax.ppermute(theirs, PLACE, exchange_route((*((ADD, 0, 1),) * 2, PACKET_ACROSS)))
    return pl.pallas_call(
        chip_kernel,
        out_shape=jax.ShapeDtypeStruct((owned, dim // 2), jnp.float32),
        in_specs=[VMEM] * (3 + len(direct) + len(passed)),
        out_specs=VMEM,
        scratch_shapes=[pltpu.VMEM((2 * cycle_size, tile_items, dim), jnp.bfloat16)],
        compiler_params=pltpu.CompilerParams(vmem_limit_bytes=8 * 1024 * 1024),
    )(*direct, *passed, mine, theirs, ridge)


def gathered_kernel(factors_ref, pair_ref, counts_ref, out_ref):
    ridge = regular_weight * counts_ref[...].astype(jnp.float32)
    total = conjugate_gradient(
        factors_ref[...], pair_ref[0].astype(jnp.float32), pair_ref[1], ridge
    )
    out_ref[...] = columns_of(total, lax.axis_index("rep"), out_ref.shape[1])


def gathered_shards(item_factors, confidence, ratings, pattern, counts):
    tile_items, dim = item_factors.shape
    groups = lax.axis_size("grp")
    group = lax.axis_index("grp")
    half = dim // lax.axis_size("rep")
    users, cycle_size = confidence.shape[:2]
    owned = users // groups

    factors = lax.all_gather(item_factors, ("grp", "blk"), axis=0, tiled=True)

    flags = (pattern[0, :, 0] != 0)[None, :, None]
    weight = jnp.where(flags, confidence, jnp.zeros_like(confidence))
    paired = (weight.astype(jnp.float32) * ratings.astype(jnp.float32)).astype(jnp.bfloat16)
    pair = jnp.stack([weight, paired]).reshape(2, groups, owned, cycle_size * tile_items)
    pieces = []
    for distance in range(groups):
        part = lax.dynamic_index_in_dim(pair, (group + distance) % groups, 1, keepdims=False)
        if distance:
            part = lax.ppermute(
                part, "grp", [(i, (i + distance) % groups) for i in range(groups)]
            )
        pieces.append(part)
    received = jnp.stack(pieces)[(group - jnp.arange(groups)) % groups]
    all_pair = jnp.moveaxis(received, 0, 2).reshape(2, owned, -1)
    owned_counts = lax.dynamic_slice_in_dim(counts, group * owned, owned, 0)[:, None]
    return pl.pallas_call(
        gathered_kernel,
        out_shape=jax.ShapeDtypeStruct((owned, half), jnp.float32),
        in_specs=[VMEM] * 3,
        out_specs=VMEM,
        compiler_params=pltpu.CompilerParams(vmem_limit_bytes=48 * 1024 * 1024),
    )(factors, all_pair, owned_counts)


def solution(mesh):
    in_specs = (
        P(("parts", "blk", "grp"), None),
        P(("parts", "blk"), None, "grp"),
        P(("parts", "blk"), None, "grp"),
        P(("parts", "blk"), None, "grp"),
        P(("parts", "blk")),
    )
    out_specs = P(("parts", "blk", "grp"), "rep")
    sizes = tuple(mesh.shape[axis] for axis in PLACE)
    shards = chip_shards if sizes == (4, 2, 2) else gathered_shards
    return jax.shard_map(shards, mesh=mesh, in_specs=in_specs, out_specs=out_specs, check_vma=False)
```

```python
import functools

import jax
import jax.numpy as jnp
from jax import lax
from jax.experimental import pallas as pl
from jax.experimental.pallas import tpu as pltpu
from jax.sharding import PartitionSpec as P

CG_STEPS = 4

unobserved_weight = 0.25
regular_weight = 0.002
epsilon = 1e-06

PLACE = ("blk", "grp", "rep")
ADD, FLIP = "add", "flip"
EXCHANGES = (
    ((FLIP, 2, 1), (ADD, 1, 0), 1),
    ((FLIP, 1, 1), (FLIP, 3, 1), 0),
    ((ADD, 2, 0), (ADD, 3, 0), 1),
)
PACKET_ACROSS = 1


def stepped(change, position, steps):
    return position ^ abs(steps) if change == FLIP else (position + steps) % 4


def exchange_route(rules):
    route = []
    *rules, across = rules
    for core, (change, steps, other) in enumerate(rules):
        for position in range(4):
            for group in range(2):
                target = stepped(change, position, steps)
                route.append(
                    (
                        (position * 2 + group) * 2 + core,
                        (target * 2 + (group ^ other)) * 2 + (core ^ across),
                    )
                )
    return route


def source_slot(rule, position):
    change, steps, other = rule
    if change == FLIP:
        source = lax.bitwise_xor(position, steps)
    else:
        source = lax.bitwise_and(position - steps, 3)
    return 4 * other + source


def halves(value):
    high = value.astype(jnp.bfloat16)
    low = (value - high.astype(jnp.float32)).astype(jnp.bfloat16)
    return jnp.concatenate([high, low], axis=0)


def joined(value, rows):
    return value[:rows] + value[rows:]


def row_sums(value):
    return jnp.sum(value, axis=1, keepdims=True)


def conjugate_gradient(factors, weighted, paired, ridge):
    rows = weighted.shape[0]
    weights = weighted + unobserved_weight

    def project(vector):
        return joined(
            lax.dot_general(
                halves(vector),
                factors,
                (((1,), (1,)), ((), ())),
                preferred_element_type=jnp.float32,
            ),
            rows,
        )

    def back(values):
        return joined(
            jnp.dot(halves(values), factors, preferred_element_type=jnp.float32),
            rows,
        )

    residual = jnp.dot(paired, factors, preferred_element_type=jnp.float32)
    direction = residual
    projected = project(residual)
    norm_now = row_sums(residual * residual)
    total = jnp.zeros_like(residual)
    for turn in range(CG_STEPS):
        weighed = weights * projected
        curvature = row_sums(weighed * projected) + ridge * row_sums(direction * direction)
        step_size = norm_now / (curvature + epsilon)
        total = total + step_size * direction
        if turn == CG_STEPS - 1:
            break
        residual = residual - step_size * (back(weighed) + ridge * direction)
        norm_next = row_sums(residual * residual)
        ratio = norm_next / (norm_now + epsilon)
        projected = project(residual) + ratio * projected
        direction = residual + ratio * direction
        norm_now = norm_next
    return total


def columns_of(total, core, half):
    chosen = total[:, :half]
    for other in range(1, total.shape[1] // half):
        chosen = jnp.where(core == other, total[:, other * half : (other + 1) * half], chosen)
    return chosen


def packet_kernel(
    flags_ref,
    confidence_ref,
    ratings_ref,
    factors_ref,
    counts_ref,
    earlier_ref,
    mine_ref,
    theirs_ref,
    ridge_ref,
    weight_ref,
    rating_ref,
    count_ref,
    flag_ref,
    value_ref,
    arrived,
):
    del earlier_ref
    group = lax.axis_index("grp")
    rows, tile_items = confidence_ref.shape
    owned = ridge_ref.shape[0]
    users = 2 * owned
    cycle_size = rows // users
    copies = [
        pltpu.make_async_copy(source, target, arrived.at[number])
        for number, (source, target) in enumerate(
            (
                (confidence_ref, weight_ref),
                (ratings_ref, rating_ref),
                (factors_ref, mine_ref.at[pl.ds(0, tile_items)]),
                (factors_ref, theirs_ref.at[pl.ds(0, tile_items)]),
                (counts_ref, count_ref),
                (flags_ref, flag_ref),
            )
        )
    ]
    for copy in copies:
        copy.start()
    copies[0].wait()
    copies[1].wait()
    copies[5].wait()
    weight = weight_ref[...].astype(jnp.float32)
    rating = rating_ref[...].astype(jnp.float32)
    source = lax.rem(lax.broadcasted_iota(jnp.int32, (rows, tile_items), 0), cycle_size)
    flag = jnp.zeros_like(source)
    for number in range(cycle_size):
        flag = jnp.where(source == number, flag_ref[number], flag)
    weight = jnp.where(flag != 0, weight, 0.0)
    for kind, value in enumerate((weight, weight * rating)):
        value_ref[kind] = value
        for number in range(cycle_size):
            target = pl.ds(tile_items + (kind * cycle_size + number) * owned, owned)
            for packet_ref, half in ((mine_ref, group), (theirs_ref, 1 - group)):
                start = half * (owned * cycle_size) + number
                packet_ref[target] = value_ref[
                    kind, pl.ds(start, owned, stride=cycle_size)
                ].astype(jnp.bfloat16)
    for copy in copies[2:5]:
        copy.wait()
    user = lax.broadcasted_iota(jnp.int32, (owned, users), 0) + group * owned
    entry = lax.broadcasted_iota(jnp.int32, user.shape, 1)
    counts = row_sums(jnp.where(user == entry, count_ref[...].astype(jnp.float32), 0.0))
    ridge_ref[...] = jnp.broadcast_to(regular_weight * counts, ridge_ref.shape)


def chip_kernel(*refs):
    *block_refs, mine_ref, theirs_ref, ridge_ref, out_ref, held = refs
    position = lax.axis_index("blk")
    core = lax.axis_index("rep")
    slots, tile_items, dim = held.shape
    owned, cycle_size = out_ref.shape[0], slots // 2
    for number, rules in enumerate(EXCHANGES):
        *rules, across = rules
        places = [source_slot(rule, position) for rule in rules]
        places = places[::-1] if across else places
        direct, passed = block_refs[number], block_refs[len(EXCHANGES) + number]
        held[jnp.where(core == 0, places[0], places[1])] = direct[...]
        held[jnp.where(core == 0, places[1], places[0])] = passed[...]
    held[position] = mine_ref[:tile_items]
    held[cycle_size + position] = theirs_ref[:tile_items]
    factors = held[...].reshape(-1, dim)

    def joined_tiles(kind):
        rows = [
            pl.ds(tile_items + (kind * cycle_size + source) * owned, owned)
            for source in range(cycle_size)
        ]
        return jnp.concatenate([ref[row] for ref in (mine_ref, theirs_ref) for row in rows], axis=1)

    weighted = joined_tiles(0).astype(jnp.float32)
    total = conjugate_gradient(factors, weighted, joined_tiles(1), ridge_ref[...])
    out_ref[...] = columns_of(total, core, out_ref.shape[1])


VMEM = pl.BlockSpec(memory_space=pltpu.VMEM)
HBM = pl.BlockSpec(memory_space=pltpu.HBM)


def chip_shards(item_factors, confidence, ratings, pattern, counts):
    tile_items, dim = item_factors.shape
    users, cycle_size = confidence.shape[:2]
    owned = users // 2
    swap = [(0, 1), (1, 0)]
    direct = [lax.ppermute(item_factors, PLACE, exchange_route(rules)) for rules in EXCHANGES]
    passed = [lax.ppermute(block, "rep", swap) for block in direct]
    rows = (users * cycle_size, tile_items)
    packet_inputs = (
        pattern[0, :, 0],
        confidence.reshape(rows),
        ratings.reshape(rows),
        item_factors,
        counts[None],
    )
    packet = jax.ShapeDtypeStruct((tile_items + 2 * cycle_size * owned, dim), jnp.bfloat16)
    ridge = jax.ShapeDtypeStruct((owned, dim), jnp.float32)
    mine, theirs, ridge = pl.pallas_call(
        packet_kernel,
        out_shape=(packet, packet, ridge),
        in_specs=[HBM] * 5 + [VMEM],
        out_specs=(VMEM, VMEM, VMEM),
        scratch_shapes=[
            pltpu.VMEM(rows, jnp.bfloat16),
            pltpu.VMEM(rows, jnp.bfloat16),
            pltpu.VMEM((1, users), jnp.int32),
            pltpu.SMEM((cycle_size,), jnp.int32),
            pltpu.VMEM((2, *rows), jnp.float32),
            pltpu.SemaphoreType.DMA((6,)),
        ],
        compiler_params=pltpu.CompilerParams(vmem_limit_bytes=8 * 1024 * 1024),
    )(
        *(pltpu.with_memory_space_constraint(array, pltpu.HBM) for array in packet_inputs), direct[0]
    )
    theirs = lax.ppermute(theirs, PLACE, exchange_route((*((ADD, 0, 1),) * 2, PACKET_ACROSS)))
    return pl.pallas_call(
        chip_kernel,
        out_shape=jax.ShapeDtypeStruct((owned, dim // 2), jnp.float32),
        in_specs=[VMEM] * (3 + len(direct) + len(passed)),
        out_specs=VMEM,
        scratch_shapes=[pltpu.VMEM((2 * cycle_size, tile_items, dim), jnp.bfloat16)],
        compiler_params=pltpu.CompilerParams(vmem_limit_bytes=8 * 1024 * 1024),
    )(*direct, *passed, mine, theirs, ridge)


def gathered_kernel(factors_ref, pair_ref, counts_ref, out_ref):
    ridge = regular_weight * counts_ref[...].astype(jnp.float32)
    total = conjugate_gradient(
        factors_ref[...], pair_ref[0].astype(jnp.float32), pair_ref[1], ridge
    )
    out_ref[...] = columns_of(total, lax.axis_index("rep"), out_ref.shape[1])


def gathered_shards(item_factors, confidence, ratings, pattern, counts):
    tile_items, dim = item_factors.shape
    groups = lax.axis_size("grp")
    group = lax.axis_index("grp")
    half = dim // lax.axis_size("rep")
    users, cycle_size = confidence.shape[:2]
    owned = users // groups

    factors = lax.all_gather(item_factors, ("grp", "blk"), axis=0, tiled=True)

    flags = (pattern[0, :, 0] != 0)[None, :, None]
    weight = jnp.where(flags, confidence, jnp.zeros_like(confidence))
    paired = (weight.astype(jnp.float32) * ratings.astype(jnp.float32)).astype(jnp.bfloat16)
    pair = jnp.stack([weight, paired]).reshape(2, groups, owned, cycle_size * tile_items)
    pieces = []
    for distance in range(groups):
        part = lax.dynamic_index_in_dim(pair, (group + distance) % groups, 1, keepdims=False)
        if distance:
            part = lax.ppermute(
                part, "grp", [(i, (i + distance) % groups) for i in range(groups)]
            )
        pieces.append(part)
    received = jnp.stack(pieces)[(group - jnp.arange(groups)) % groups]
    all_pair = jnp.moveaxis(received, 0, 2).reshape(2, owned, -1)
    owned_counts = lax.dynamic_slice_in_dim(counts, group * owned, owned, 0)[:, None]
    return pl.pallas_call(
        gathered_kernel,
        out_shape=jax.ShapeDtypeStruct((owned, half), jnp.float32),
        in_specs=[VMEM] * 3,
        out_specs=VMEM,
        compiler_params=pltpu.CompilerParams(vmem_limit_bytes=48 * 1024 * 1024),
    )(factors, all_pair, owned_counts)


def solution(mesh):
    in_specs = (
        P(("parts", "blk", "grp"), None),
        P(("parts", "blk"), None, "grp"),
        P(("parts", "blk"), None, "grp"),
        P(("parts", "blk"), None, "grp"),
        P(("parts", "blk")),
    )
    out_specs = P(("parts", "blk", "grp"), "rep")
    sizes = tuple(mesh.shape[axis] for axis in PLACE)
    shards = chip_shards if sizes == (4, 2, 2) else gathered_shards
    return jax.shard_map(shards, mesh=mesh, in_specs=in_specs, out_specs=out_specs, check_vma=False)
```

```python
import functools

import jax
import jax.numpy as jnp
from jax import lax
from jax.experimental import pallas as pl
from jax.experimental.pallas import tpu as pltpu
from jax.sharding import PartitionSpec as P

CG_STEPS = 4

unobserved_weight = 0.25
regular_weight = 0.002
epsilon = 1e-06

PLACE = ("blk", "grp", "rep")
ADD, FLIP = "add", "flip"
EXCHANGES = (
    ((FLIP, 2, 1), (ADD, 1, 0), 1),
    ((FLIP, 1, 1), (FLIP, 3, 1), 0),
    ((ADD, 2, 0), (ADD, 3, 0), 1),
)
PACKET_ACROSS = 1


def stepped(change, position, steps):
    return position ^ abs(steps) if change == FLIP else (position + steps) % 4


def exchange_route(rules):
    route = []
    *rules, across = rules
    for core, (change, steps, other) in enumerate(rules):
        for position in range(4):
            for group in range(2):
                target = stepped(change, position, steps)
                route.append(
                    (
                        (position * 2 + group) * 2 + core,
                        (target * 2 + (group ^ other)) * 2 + (core ^ across),
                    )
                )
    return route


def source_slot(rule, position):
    change, steps, other = rule
    if change == FLIP:
        source = lax.bitwise_xor(position, steps)
    else:
        source = lax.bitwise_and(position - steps, 3)
    return 4 * other + source


def halves(value):
    high = value.astype(jnp.bfloat16)
    low = (value - high.astype(jnp.float32)).astype(jnp.bfloat16)
    return jnp.concatenate([high, low], axis=0)


def joined(value, rows):
    return value[:rows] + value[rows:]


def row_sums(value):
    return jnp.sum(value, axis=1, keepdims=True)


def conjugate_gradient(factors, weighted, paired, ridge):
    rows = weighted.shape[0]
    weights = weighted + unobserved_weight

    def project(vector):
        return joined(
            lax.dot_general(
                halves(vector),
                factors,
                (((1,), (1,)), ((), ())),
                preferred_element_type=jnp.float32,
            ),
            rows,
        )

    def back(values):
        return joined(
            jnp.dot(halves(values), factors, preferred_element_type=jnp.float32),
            rows,
        )

    residual = jnp.dot(paired, factors, preferred_element_type=jnp.float32)
    direction = residual
    projected = project(residual)
    norm_now = row_sums(residual * residual)
    total = jnp.zeros_like(residual)
    for turn in range(CG_STEPS):
        weighed = weights * projected
        curvature = row_sums(weighed * projected) + ridge * row_sums(direction * direction)
        step_size = norm_now / (curvature + epsilon)
        total = total + step_size * direction
        if turn == CG_STEPS - 1:
            break
        residual = residual - step_size * (back(weighed) + ridge * direction)
        norm_next = row_sums(residual * residual)
        ratio = norm_next / (norm_now + epsilon)
        projected = project(residual) + ratio * projected
        direction = residual + ratio * direction
        norm_now = norm_next
    return total


def columns_of(total, core, half):
    chosen = total[:, :half]
    for other in range(1, total.shape[1] // half):
        chosen = jnp.where(core == other, total[:, other * half : (other + 1) * half], chosen)
    return chosen


def packet_kernel(
    flags_ref,
    confidence_ref,
    ratings_ref,
    factors_ref,
    counts_ref,
    earlier_ref,
    mine_ref,
    theirs_ref,
    ridge_ref,
    weight_ref,
    rating_ref,
    count_ref,
    flag_ref,
    value_ref,
    arrived,
):
    del earlier_ref
    group = lax.axis_index("grp")
    rows, tile_items = confidence_ref.shape
    owned = ridge_ref.shape[0]
    users = 2 * owned
    cycle_size = rows // users
    copies = [
        pltpu.make_async_copy(source, target, arrived.at[number])
        for number, (source, target) in enumerate(
            (
                (confidence_ref, weight_ref),
                (ratings_ref, rating_ref),
                (factors_ref, mine_ref.at[pl.ds(0, tile_items)]),
                (factors_ref, theirs_ref.at[pl.ds(0, tile_items)]),
                (counts_ref, count_ref),
                (flags_ref, flag_ref),
            )
        )
    ]
    for copy in copies:
        copy.start()
    copies[0].wait()
    copies[1].wait()
    copies[5].wait()
    weight = weight_ref[...].astype(jnp.float32)
    rating = rating_ref[...].astype(jnp.float32)
    source = lax.rem(lax.broadcasted_iota(jnp.int32, (rows, tile_items), 0), cycle_size)
    flag = jnp.zeros_like(source)
    for number in range(cycle_size):
        flag = jnp.where(source == number, flag_ref[number], flag)
    weight = jnp.where(flag != 0, weight, 0.0)
    for kind, value in enumerate((weight, weight * rating)):
        value_ref[kind] = value
        for number in range(cycle_size):
            target = pl.ds(tile_items + (kind * cycle_size + number) * owned, owned)
            for packet_ref, half in ((mine_ref, group), (theirs_ref, 1 - group)):
                start = half * (owned * cycle_size) + number
                packet_ref[target] = value_ref[
                    kind, pl.ds(start, owned, stride=cycle_size)
                ].astype(jnp.bfloat16)
    for copy in copies[2:5]:
        copy.wait()
    user = lax.broadcasted_iota(jnp.int32, (owned, users), 0) + group * owned
    entry = lax.broadcasted_iota(jnp.int32, user.shape, 1)
    counts = row_sums(jnp.where(user == entry, count_ref[...].astype(jnp.float32), 0.0))
    ridge_ref[...] = jnp.broadcast_to(regular_weight * counts, ridge_ref.shape)


def chip_kernel(*refs):
    *block_refs, mine_ref, theirs_ref, ridge_ref, out_ref = refs
    position = lax.axis_index("blk")
    core = lax.axis_index("rep")
    tile_items = block_refs[0].shape[0]
    owned = out_ref.shape[0]
    cycle_size = (mine_ref.shape[0] - tile_items) // (2 * owned)
    blocks = [mine_ref[:tile_items], theirs_ref[:tile_items]]
    slots = [position, cycle_size + position]
    for number, rules in enumerate(EXCHANGES):
        *rules, across = rules
        places = [source_slot(rule, position) for rule in rules]
        places = places[::-1] if across else places
        blocks += [block_refs[number][...], block_refs[len(EXCHANGES) + number][...]]
        slots += [
            jnp.where(core == 0, places[0], places[1]),
            jnp.where(core == 0, places[1], places[0]),
        ]
    factors = jnp.concatenate(blocks, axis=0)

    def joined_tiles(kind):
        tiles = []
        for slot in slots:
            source = lax.rem(slot, cycle_size)
            start = tile_items + (kind * cycle_size + source) * owned
            rows = pl.ds(pl.multiple_of(start, owned), owned)
            tiles.append(jnp.where(slot < cycle_size, mine_ref[rows], theirs_ref[rows]))
        return jnp.concatenate(tiles, axis=1)

    weighted = joined_tiles(0).astype(jnp.float32)
    total = conjugate_gradient(factors, weighted, joined_tiles(1), ridge_ref[...])
    out_ref[...] = columns_of(total, core, out_ref.shape[1])


VMEM = pl.BlockSpec(memory_space=pltpu.VMEM)
HBM = pl.BlockSpec(memory_space=pltpu.HBM)


def chip_shards(item_factors, confidence, ratings, pattern, counts):
    tile_items, dim = item_factors.shape
    users, cycle_size = confidence.shape[:2]
    owned = users // 2
    swap = [(0, 1), (1, 0)]
    direct = [lax.ppermute(item_factors, PLACE, exchange_route(rules)) for rules in EXCHANGES]
    passed = [lax.ppermute(block, "rep", swap) for block in direct]
    rows = (users * cycle_size, tile_items)
    packet_inputs = (
        pattern[0, :, 0],
        confidence.reshape(rows),
        ratings.reshape(rows),
        item_factors,
        counts[None],
    )
    packet = jax.ShapeDtypeStruct((tile_items + 2 * cycle_size * owned, dim), jnp.bfloat16)
    ridge = jax.ShapeDtypeStruct((owned, dim), jnp.float32)
    mine, theirs, ridge = pl.pallas_call(
        packet_kernel,
        out_shape=(packet, packet, ridge),
        in_specs=[HBM] * 5 + [VMEM],
        out_specs=(VMEM, VMEM, VMEM),
        scratch_shapes=[
            pltpu.VMEM(rows, jnp.bfloat16),
            pltpu.VMEM(rows, jnp.bfloat16),
            pltpu.VMEM((1, users), jnp.int32),
            pltpu.SMEM((cycle_size,), jnp.int32),
            pltpu.VMEM((2, *rows), jnp.float32),
            pltpu.SemaphoreType.DMA((6,)),
        ],
        compiler_params=pltpu.CompilerParams(vmem_limit_bytes=8 * 1024 * 1024),
    )(
        *(pltpu.with_memory_space_constraint(array, pltpu.HBM) for array in packet_inputs), direct[0]
    )
    theirs = lax.ppermute(theirs, PLACE, exchange_route((*((ADD, 0, 1),) * 2, PACKET_ACROSS)))
    return pl.pallas_call(
        chip_kernel,
        out_shape=jax.ShapeDtypeStruct((owned, dim // 2), jnp.float32),
        in_specs=[VMEM] * (3 + len(direct) + len(passed)),
        out_specs=VMEM,
        compiler_params=pltpu.CompilerParams(vmem_limit_bytes=8 * 1024 * 1024),
    )(*direct, *passed, mine, theirs, ridge)


def gathered_kernel(factors_ref, pair_ref, counts_ref, out_ref):
    ridge = regular_weight * counts_ref[...].astype(jnp.float32)
    total = conjugate_gradient(
        factors_ref[...], pair_ref[0].astype(jnp.float32), pair_ref[1], ridge
    )
    out_ref[...] = columns_of(total, lax.axis_index("rep"), out_ref.shape[1])


def gathered_shards(item_factors, confidence, ratings, pattern, counts):
    tile_items, dim = item_factors.shape
    groups = lax.axis_size("grp")
    group = lax.axis_index("grp")
    half = dim // lax.axis_size("rep")
    users, cycle_size = confidence.shape[:2]
    owned = users // groups

    factors = lax.all_gather(item_factors, ("grp", "blk"), axis=0, tiled=True)

    flags = (pattern[0, :, 0] != 0)[None, :, None]
    weight = jnp.where(flags, confidence, jnp.zeros_like(confidence))
    paired = (weight.astype(jnp.float32) * ratings.astype(jnp.float32)).astype(jnp.bfloat16)
    pair = jnp.stack([weight, paired]).reshape(2, groups, owned, cycle_size * tile_items)
    pieces = []
    for distance in range(groups):
        part = lax.dynamic_index_in_dim(pair, (group + distance) % groups, 1, keepdims=False)
        if distance:
            part = lax.ppermute(
                part, "grp", [(i, (i + distance) % groups) for i in range(groups)]
            )
        pieces.append(part)
    received = jnp.stack(pieces)[(group - jnp.arange(groups)) % groups]
    all_pair = jnp.moveaxis(received, 0, 2).reshape(2, owned, -1)
    owned_counts = lax.dynamic_slice_in_dim(counts, group * owned, owned, 0)[:, None]
    return pl.pallas_call(
        gathered_kernel,
        out_shape=jax.ShapeDtypeStruct((owned, half), jnp.float32),
        in_specs=[VMEM] * 3,
        out_specs=VMEM,
        compiler_params=pltpu.CompilerParams(vmem_limit_bytes=48 * 1024 * 1024),
    )(factors, all_pair, owned_counts)


def solution(mesh):
    in_specs = (
        P(("parts", "blk", "grp"), None),
        P(("parts", "blk"), None, "grp"),
        P(("parts", "blk"), None, "grp"),
        P(("parts", "blk"), None, "grp"),
        P(("parts", "blk")),
    )
    out_specs = P(("parts", "blk", "grp"), "rep")
    sizes = tuple(mesh.shape[axis] for axis in PLACE)
    shards = chip_shards if sizes == (4, 2, 2) else gathered_shards
    return jax.shard_map(shards, mesh=mesh, in_specs=in_specs, out_specs=out_specs, check_vma=False)
```
